32 devices in a mesh: step: 4 (over y, x), frame: 8 (over z, core).
Axes of the slice: x: 2, y: 2, z: 4, core: 2. Of those that a mesh axis runs over, the one named last changes fastest.
Arguments:
- start_state: bfloat16 [8, 32, 32, 320], P('frame'), may hold values from -6 to 6
- step_noise: bfloat16 [4, 8, 32, 32, 320], P('step', 'frame'), may hold values from -6 to 6
- timesteps: int32 [4], P('step'), may hold values from 0 to 999
- gn_gain: float32 [320], replicated, may hold values from 0.1 to 1.9
- gn_bias: float32 [320], replicated, may hold values from -3 to 3
- spatial_weight: bfloat16 [3, 3, 320, 320], replicated, may hold values from -0.109375 to 0.109375
- temporal_weight: bfloat16 [3, 320, 320], replicated, may hold values from -0.1875 to 0.1875
- temb_weight: bfloat16 [320, 320], replicated, may hold values from -0.3125 to 0.3125
Outputs:
- next_states: bfloat16 [4, 8, 32, 32, 320], P('step', 'frame')
The draws below stay inside these ranges and needn't reach their ends.
All inputs are finite; a program needn't handle non-finite values.
Results may differ from the reference program's by a relative error of at most 0.005.
Values may be sent and summed in bfloat16 or wider, within the bound.
A program may use at most 128 MiB of HBM per device.

```python
import math
import jax
import jax.numpy as jnp
from jax import lax

C = 320
TEMB = 320
GROUPS = 32
H = 32
W = 32
STEPS = 4
FRAMES = 8


def place_ends(array, rng, least, high):
    longest = array.shape.index(max(array.shape))
    spots = []
    for shift in (0, 1):
        where = [jax.random.randint(jax.random.fold_in(rng, axis), (), 0, length) for axis, length in enumerate(array.shape)]
        where[longest] = (where[longest] + shift) % array.shape[longest]
        spots.append(tuple(where))
    return array.at[spots[0]].set(least).at[spots[1]].set(high)


def block_scale(stream_key, dims, pieces, low, top_value):
    level = 1.0
    for axis_at, parts in pieces:
        steps = jax.random.uniform(jax.random.fold_in(jax.random.fold_in(stream_key, 6), axis_at), (parts,), jnp.float32, low / len(pieces), top_value / len(pieces))
        level = level * jnp.repeat(jnp.exp(steps), dims[axis_at] // parts).reshape((-1,) + (1,) * (len(dims) - 1 - axis_at))
    return level


def scatter_about(rng, shape, deviation, most, pieces=(), kind=jnp.bfloat16):
    array = jax.random.normal(rng, shape, jnp.float32) * deviation
    if len(pieces) > 0:
        array = block_scale(rng, shape, pieces, -0.22, 0.18) * array
    return jnp.clip(array, min=-most, max=most).astype(kind)


def setup_inputs(seed: int = 0) -> dict:
    arg_keys = jax.random.split(jax.random.key(seed), 9)
    return {
        "start_state": scatter_about(arg_keys[0], (FRAMES, H, W, C), 1.0, 6.0, ((0, 8),)),
        "step_noise": scatter_about(arg_keys[1], (STEPS, FRAMES, H, W, C), 1.0, 6.0, ((0, 4), (1, 8))),
        "timesteps": place_ends(jax.random.randint(arg_keys[2], (STEPS,), 0, 1000), jax.random.fold_in(arg_keys[2], 1), 0, 999).astype(jnp.int32),
        "gn_gain": jnp.clip(1.0 + 0.18 * jax.random.normal(arg_keys[3], (C,), jnp.float32), 0.1, 1.9),
        "gn_bias": scatter_about(arg_keys[4], (C,), 0.5, 3.0, (), jnp.float32),
        "spatial_weight": scatter_about(arg_keys[5], (3, 3, C, C), (9 * C) ** -0.5, 0.109375),
        "temporal_weight": scatter_about(arg_keys[6], (3, C, C), (3 * C) ** -0.5, 0.1875),
        "temb_weight": scatter_about(arg_keys[7], (TEMB, C), TEMB ** -0.5, 0.3125),
    }


def norm_silu(current, gn_gain, gn_bias):
    frames_here, rows, columns, channels = current.shape
    grouped = current.astype(jnp.float32).reshape(frames_here, rows, columns, GROUPS, channels // GROUPS)
    group_mean = lax.optimization_barrier(jnp.mean(grouped, axis=(1, 2, 4), keepdims=True))
    centered = grouped - group_mean
    group_var = lax.optimization_barrier(jnp.mean(centered * centered, axis=(1, 2, 4), keepdims=True))
    scaled = (centered * lax.rsqrt(group_var + 1e-05)).reshape(frames_here, rows, columns, channels)
    return jax.nn.silu(scaled * gn_gain + gn_bias).astype(jnp.bfloat16)

def time_vector(step_index, temb_weight):
    half_dim = temb_weight.shape[0] // 2
    frequencies = jnp.exp(-math.log(10000.0) * jnp.arange(half_dim, dtype=jnp.float32) / half_dim)
    angles = step_index.astype(jnp.float32) * frequencies
    embedding = jnp.concatenate([jnp.cos(angles), jnp.sin(angles)]).astype(jnp.bfloat16)
    return jax.nn.silu(jnp.dot(embedding, temb_weight, preferred_element_type=jnp.float32))

def spatial_conv(normed, spatial_weight):
    rows, columns = (normed.shape[1], normed.shape[2])
    padded = jnp.pad(normed, ((0, 0), (1, 1), (1, 1), (0, 0)))
    total = None
    for row_off in range(3):
        for col_off in range(3):
            window = padded[:, row_off:row_off + rows, col_off:col_off + columns, :]
            term = jnp.dot(window, spatial_weight[row_off, col_off], preferred_element_type=jnp.float32)
            total = term if total is None else total + term
    return total

def frame_conv(extended, temporal_weight, frames_out):
    total = None
    for offset in range(3):
        term = jnp.dot(extended[offset:offset + frames_out], temporal_weight[offset], preferred_element_type=jnp.float32)
        total = term if total is None else total + term
    return total.astype(jnp.bfloat16)

def reference(start_state, step_noise, timesteps, gn_gain, gn_bias, spatial_weight, temporal_weight, temb_weight):
    frame_count = start_state.shape[0]

    def drift_one(inputs):
        current, noise_now, step_index = inputs
        normed = norm_silu(current, gn_gain, gn_bias)
        time_bias = time_vector(step_index, temb_weight)
        activated = jax.nn.silu(spatial_conv(normed, spatial_weight) + time_bias).astype(jnp.bfloat16)
        extended = jnp.pad(activated, ((1, 1), (0, 0), (0, 0), (0, 0)))
        update = frame_conv(extended, temporal_weight, frame_count)
        return 0.25 * update.astype(jnp.float32) + 0.25 * noise_now.astype(jnp.float32)
    start_wide = start_state.astype(jnp.float32)
    first_states = jnp.broadcast_to(start_state, (STEPS,) + start_state.shape)
    first_drift = lax.map(drift_one, (first_states, step_noise, timesteps))
    inclusive = jnp.cumsum(first_drift, axis=0)
    exclusive = jnp.concatenate([jnp.zeros_like(inclusive[:1]), inclusive[:-1]], axis=0)
    states = (start_wide + exclusive).astype(jnp.bfloat16)
    second_drift = lax.map(drift_one, (states, step_noise, timesteps))
    return (start_wide + jnp.cumsum(second_drift, axis=0)).astype(jnp.bfloat16)
```

```python
import math

import jax
import jax.numpy as jnp
from jax import lax
from jax.sharding import PartitionSpec as P

GROUPS = 32


def extended_2(cells, sides, width):
    for axis, dim in sides:
        count = lax.axis_size(axis)
        ends = count - 1
        head = lax.slice_in_dim(cells, 0, width, axis=dim)
        tail = lax.slice_in_dim(cells, cells.shape[dim] - width, cells.shape[dim], axis=dim)
        cells = jnp.concatenate(
            [
                lax.ppermute(tail, axis, [(i, (i + 1) % count) for i in range(ends)]),
                cells,
                lax.ppermute(head, axis, [((i + 1) % count, i) for i in range(ends)]),
            ],
            axis=dim,
        )
    return cells


def prefix(part, axis):
    count = lax.axis_size(axis)
    place = lax.axis_index(axis)
    wide = part.astype(jnp.float32)
    before = jnp.zeros_like(wide)
    total = wide
    hop = 1
    while hop < count:
        pairs = [(i, i ^ hop) for i in range(count) if 2 * hop < count or not i & hop]
        got = lax.ppermute(total.astype(jnp.bfloat16), axis, pairs).astype(jnp.float32)
        before = before + jnp.where((place & hop) != 0, got, 0.0)
        total = total + got
        hop *= 2
    return before


def norm_silu(current, gn_gain, gn_bias):
    frames_here, rows, columns, channels = current.shape
    grouped = current.astype(jnp.float32).reshape(
        frames_here, rows, columns, GROUPS, channels // GROUPS
    )
    group_mean = jnp.mean(grouped, axis=(1, 2, 4), keepdims=True)
    centered = grouped - group_mean
    group_var = jnp.mean(centered * centered, axis=(1, 2, 4), keepdims=True)
    scaled = (centered * lax.rsqrt(group_var + 1e-05)).reshape(frames_here, rows, columns, channels)
    return jax.nn.silu(scaled * gn_gain + gn_bias).astype(jnp.bfloat16)


def time_vector(step_index, temb_weight):
    half_dim = temb_weight.shape[0] // 2
    frequencies = jnp.exp(-math.log(10000.0) * jnp.arange(half_dim, dtype=jnp.float32) / half_dim)
    angles = step_index.astype(jnp.float32) * frequencies
    embedding = jnp.concatenate([jnp.cos(angles), jnp.sin(angles)]).astype(jnp.bfloat16)
    return jax.nn.silu(jnp.dot(embedding, temb_weight, preferred_element_type=jnp.float32))


def spatial_conv(normed, spatial_weight):
    rows, columns = (normed.shape[1], normed.shape[2])
    padded = jnp.pad(normed, ((0, 0), (1, 1), (1, 1), (0, 0)))
    total = None
    for row_off in range(3):
        for col_off in range(3):
            window = padded[:, row_off : row_off + rows, col_off : col_off + columns, :]
            term = jnp.dot(
                window, spatial_weight[row_off, col_off], preferred_element_type=jnp.float32
            )
            total = term if total is None else total + term
    return total


def frame_conv(extended, temporal_weight, frames_out):
    total = None
    for offset in range(3):
        term = jnp.dot(
            extended[offset : offset + frames_out],
            temporal_weight[offset],
            preferred_element_type=jnp.float32,
        )
        total = term if total is None else total + term
    return total.astype(jnp.bfloat16)


def local(
    start_state,
    step_noise,
    timesteps,
    gn_gain,
    gn_bias,
    spatial_weight,
    temporal_weight,
    temb_weight,
):
    place = lax.axis_index("step")
    count = lax.axis_size("step")
    steps = lax.all_gather(timesteps[0], "step")
    biases = [time_vector(steps[s], temb_weight) for s in range(count)]
    own_bias = time_vector(timesteps[0], temb_weight)
    noise_before = prefix(step_noise[0], "step")
    start_wide = start_state.astype(jnp.float32)
    conv = spatial_conv(norm_silu(start_state, gn_gain, gn_bias), spatial_weight)
    activated = jnp.zeros_like(conv)
    for s in range(count - 1):
        activated += jnp.where(s < place, jax.nn.silu(conv + biases[s]), 0.0)
    extended = extended_2(activated.astype(jnp.bfloat16), (("frame", 0),), 1)
    update = frame_conv(extended, temporal_weight, 1).astype(jnp.float32)
    current = (start_wide + 0.25 * (update + noise_before)).astype(jnp.bfloat16)
    conv = spatial_conv(norm_silu(current, gn_gain, gn_bias), spatial_weight)
    activated = jax.nn.silu(conv + own_bias).astype(jnp.bfloat16)
    extended = extended_2(activated, (("frame", 0),), 1)
    update = frame_conv(extended, temporal_weight, 1)
    drift = update.astype(jnp.float32) + step_noise[0].astype(jnp.float32)
    result = (start_wide + 0.25 * (noise_before + drift + prefix(update, "step"))).astype(jnp.bfloat16)
    return result[None]


def solution(mesh):
    placed = (
        P("frame", None, None, None),
        P("step", "frame", None, None, None),
        P("step"),
        P(),
        P(),
        P(),
        P(),
        P(),
    )
    return jax.shard_map(
        local,
        mesh=mesh,
        in_specs=placed,
        out_specs=P("step", "frame", None, None, None),
        check_vma=False,
    )
```

```python
import functools
import math

import jax
import jax.numpy as jnp
from jax import lax
from jax.experimental import pallas as pl
from jax.experimental.pallas import tpu as pltpu
from jax.sharding import PartitionSpec as P

GROUPS = 32
CHUNKS = 4
MESH = pl.DeviceIdType.MESH
F32 = jnp.float32
BF16 = jnp.bfloat16


def silu(x):
    half = 0.5 * x
    return half + half * jnp.tanh(half)


def kernel(
    steps, frames, width,
    start, noise, when, gain, bias, sw, tw, tbw, out,
    tb_own, tb_all, same, x, state, act, act2, halo, upd, ntot, utot, nrecv, urecv,
    tb_send, tb_recv, h_send, h_recv, n_send, n_recv, u_send, u_recv,
):
    t = lax.axis_index("step")
    f = lax.axis_index("frame")
    cells, chan = start.shape
    size = cells // CHUNKS
    phases = len(range(0, steps.bit_length() - 1))
    has_left = f > 0
    has_right = f < frames - 1

    barrier = pltpu.get_barrier_semaphore()
    for d in range(1, steps):
        pl.semaphore_signal(barrier, inc=1, device_id=(lax.rem(t + d, steps), f), device_id_type=MESH)

    @pl.when(has_left)
    def _():
        pl.semaphore_signal(barrier, inc=1, device_id=(t, f - 1), device_id_type=MESH)

    @pl.when(has_right)
    def _():
        pl.semaphore_signal(barrier, inc=1, device_id=(t, f + 1), device_id_type=MESH)

    pl.semaphore_wait(barrier, steps - 1 + jnp.where(has_left, 1, 0) + jnp.where(has_right, 1, 0))

    def rows(c):
        return pl.ds(c * size, size)

    def bit(p):
        return lax.rem(t // (1 << p), 2)

    def swap(kind, p, c):
        own, tot, recv, ss, rs = (
            (noise, ntot, nrecv, n_send, n_recv) if kind == 0 else (upd, utot, urecv, u_send, u_recv)
        )
        src = own.at[rows(c)] if p == 0 else tot.at[p - 1, rows(c)]
        partner = t + (1 << p) * (1 - 2 * bit(p))
        return pltpu.make_async_remote_copy(
            src_ref=src, dst_ref=recv.at[p, rows(c)], send_sem=ss.at[p, c], recv_sem=rs.at[p, c],
            device_id=(partner, f), device_id_type=MESH,
        )

    def swap_do(kind, p, c, what):
        if p < phases - 1:
            what[0](swap(kind, p, c))
            return

        @pl.when(bit(p) == (0 if what[1] == "send" else 1))
        def _():
            what[0](swap(kind, p, c))

    begin = (lambda r: r.start(), "send")
    sent = (lambda r: r.wait_send(), "send")
    got = (lambda r: r.wait_recv(), "recv")

    def advance(kind, p, c):
        own, tot, recv = (noise, ntot, nrecv) if kind == 0 else (upd, utot, urecv)
        swap_do(kind, p, c, got)
        if p < phases - 1:
            have = own[rows(c), :] if p == 0 else tot[p - 1, rows(c), :]
            tot[p, rows(c), :] = (have.astype(F32) + recv[p, rows(c), :].astype(F32)).astype(BF16)
            swap_do(kind, p + 1, c, begin)

    def before(kind, c):
        recv = nrecv if kind == 0 else urecv
        total = jnp.zeros((size, chan), F32)
        for p in range(phases):
            total = total + jnp.where(bit(p) == 1, recv[p, rows(c), :].astype(F32), 0.0)
        return total

    def halo_copy(sweep, side, c):
        src = (act if sweep == 0 else act2).at[rows(c)]
        to = f + 1 if side == 0 else f - 1
        return pltpu.make_async_remote_copy(
            src_ref=src, dst_ref=halo.at[sweep, side, rows(c)],
            send_sem=h_send.at[sweep, side, c], recv_sem=h_recv.at[sweep, side, c],
            device_id=(t, to), device_id_type=MESH,
        )

    def halo_do(sweep, c, what):
        send = what[1] == "send"
        for side, cond in ((0, has_right if send else has_left), (1, has_left if send else has_right)):
            @pl.when(cond)
            def _():
                what[0](halo_copy(sweep, side, c))

    for c in range(CHUNKS):
        swap_do(0, 0, c, begin)

    lane = lax.broadcasted_iota(jnp.int32, (8, chan), 1)
    half = tbw.shape[0] // 2
    k = jnp.where(lane < half, lane, lane - half).astype(F32)
    angle = when[0].astype(F32) * jnp.exp(-math.log(10000.0) * k / half)
    emb = jnp.where(lane < half, jnp.cos(angle), jnp.sin(angle)).astype(BF16)
    tb_own[...] = silu(jnp.dot(emb, tbw[...], preferred_element_type=F32))

    def tb_copy(d):
        return pltpu.make_async_remote_copy(
            src_ref=tb_own, dst_ref=tb_all.at[d], send_sem=tb_send.at[d], recv_sem=tb_recv.at[d],
            device_id=(lax.rem(t + d, steps), f), device_id_type=MESH,
        )

    for d in range(1, steps):
        tb_copy(d).start()

    per = chan // GROUPS
    same[...] = jnp.where(
        lax.broadcasted_iota(jnp.int32, (chan, chan), 0) // per
        == lax.broadcasted_iota(jnp.int32, (chan, chan), 1) // per, 1.0, 0.0,
    ).astype(BF16)
    pad = jnp.zeros((width, x.shape[1]), BF16)
    x[pl.ds(0, width), :] = pad
    x[pl.ds(cells + width, width), :] = pad
    for sweep in range(2):
        @pl.when(jnp.logical_not(has_left))
        def _():
            halo[sweep, 0] = jnp.zeros((cells, chan), BF16)

        @pl.when(jnp.logical_not(has_right))
        def _():
            halo[sweep, 1] = jnp.zeros((cells, chan), BF16)

    @pl.when(bit(phases - 1) == 0)
    def _():
        nrecv[phases - 1] = jnp.zeros((cells, chan), BF16)
        urecv[phases - 1] = jnp.zeros((cells, chan), BF16)

    def group_mean(total):
        row = lax.broadcasted_iota(jnp.int32, (16, chan), 0)
        hi = total.astype(BF16).astype(F32)
        mid = (total - hi).astype(BF16).astype(F32)
        low = total - hi - mid
        parts = jnp.where(row == 0, hi, jnp.where(row == 1, mid, jnp.where(row == 2, low, 0.0)))
        summed = jnp.dot(parts.astype(BF16), same[...], preferred_element_type=F32)
        return jnp.sum(summed, axis=0, keepdims=True) / (per * cells)

    def fill(ref, total):
        mean = group_mean(total)
        var = jnp.zeros((1, chan), F32)
        for c in range(CHUNKS):
            centered = ref[rows(c), :].astype(F32) - mean
            var = var + jnp.sum(centered * centered, axis=0, keepdims=True)
        scale = lax.rsqrt(group_mean(var) + 1e-05) * gain[...]
        col = lax.rem(lax.broadcasted_iota(jnp.int32, (size, chan), 0), width)
        for c in range(CHUNKS):
            y = silu((ref[rows(c), :].astype(F32) - mean) * scale + bias[...])
            left = jnp.where(col == 0, 0.0, pltpu.roll(y, 1, 0))
            right = jnp.where(col == width - 1, 0.0, pltpu.roll(y, size - 1, 0))
            x[pl.ds(width + c * size, size), :] = jnp.concatenate([left, y, right], axis=1).astype(BF16)

    def conv(c):
        total = None
        for i in range(3):
            term = jnp.dot(x[pl.ds(c * size + i * width, size), :], sw[i], preferred_element_type=F32)
            total = term if total is None else total + term
        return total

    def temporal(sweep, c):
        halo_do(sweep, c, got)
        mine = act if sweep == 0 else act2
        total = jnp.dot(mine[rows(c), :], tw[1], preferred_element_type=F32)
        total = total + jnp.dot(halo[sweep, 0, rows(c), :], tw[0], preferred_element_type=F32)
        return total + jnp.dot(halo[sweep, 1, rows(c), :], tw[2], preferred_element_type=F32)

    total = jnp.zeros((1, chan), F32)
    for c in range(CHUNKS):
        total = total + jnp.sum(start[rows(c), :].astype(F32), axis=0, keepdims=True)
    fill(start, total)
    for d in range(1, steps):
        tb_copy(d).wait()
    for c in range(CHUNKS):
        acc = conv(c)
        summed = jnp.zeros_like(acc)
        for d in range(1, steps):
            summed = summed + jnp.where(d <= t, silu(acc + tb_all[d, 0:1, :]), 0.0)
        act[rows(c), :] = summed.astype(BF16)
        halo_do(0, c, begin)
        if c > 0:
            advance(0, 0, c - 1)
    advance(0, 0, CHUNKS - 1)
    for p in range(1, phases - 1):
        for c in range(CHUNKS):
            advance(0, p, c)
    total = jnp.zeros((1, chan), F32)
    for c in range(CHUNKS):
        update = temporal(0, c)
        if phases > 1:
            advance(0, phases - 1, c)
        now = (start[rows(c), :].astype(F32) + 0.25 * (update + before(0, c))).astype(BF16)
        state[rows(c), :] = now
        total = total + jnp.sum(now.astype(F32), axis=0, keepdims=True)

    fill(state, total)

    def second(c):
        upd[rows(c), :] = temporal(1, c).astype(BF16)
        swap_do(1, 0, c, begin)

    for c in range(CHUNKS):
        act2[rows(c), :] = silu(conv(c) + tb_own[0:1, :]).astype(BF16)
        halo_do(1, c, begin)
        if c > 1:
            second(c - 2)
    for c in range(CHUNKS - 2, CHUNKS):
        second(c)
        advance(1, 0, c - CHUNKS + 2)
    for c in range(2, CHUNKS):
        advance(1, 0, c)
    for p in range(1, phases - 1):
        for c in range(CHUNKS):
            advance(1, p, c)
    for c in range(CHUNKS):
        if phases > 1:
            advance(1, phases - 1, c)
        drift = before(0, c) + noise[rows(c), :].astype(F32) + before(1, c) + upd[rows(c), :].astype(F32)
        out[rows(c), :] = (start[rows(c), :].astype(F32) + 0.25 * drift).astype(BF16)

    for c in range(CHUNKS):
        for sweep in range(2):
            halo_do(sweep, c, sent)
        for kind in range(2):
            for p in range(phases):
                swap_do(kind, p, c, sent)


def local(steps, frames, start, noise, when, gain, bias, sw, tw, tbw):
    _, height, width, chan = start.shape
    cells = height * width
    phases = steps.bit_length() - 1
    big = (cells, chan)
    vm = pl.BlockSpec(memory_space=pltpu.VMEM)
    dma = pltpu.SemaphoreType.DMA
    out = pl.pallas_call(
        functools.partial(kernel, steps, frames, width),
        out_shape=jax.ShapeDtypeStruct(big, BF16),
        in_specs=[vm, vm, pl.BlockSpec(memory_space=pltpu.SMEM)] + [vm] * 5,
        out_specs=vm,
        scratch_shapes=[
            pltpu.VMEM((8, chan), F32),
            pltpu.VMEM((steps, 8, chan), F32),
            pltpu.VMEM((chan, chan), BF16),
            pltpu.VMEM((cells + 2 * width, 3 * chan), BF16),
            pltpu.VMEM(big, BF16),
            pltpu.VMEM(big, BF16),
            pltpu.VMEM(big, BF16),
            pltpu.VMEM((2, 2) + big, BF16),
            pltpu.VMEM(big, BF16),
            pltpu.VMEM((max(phases - 1, 1),) + big, BF16),
            pltpu.VMEM((max(phases - 1, 1),) + big, BF16),
            pltpu.VMEM((phases,) + big, BF16),
            pltpu.VMEM((phases,) + big, BF16),
            dma((steps,)), dma((steps,)),
            dma((2, 2, CHUNKS)), dma((2, 2, CHUNKS)),
            dma((phases, CHUNKS)), dma((phases, CHUNKS)),
            dma((phases, CHUNKS)), dma((phases, CHUNKS)),
        ],
        compiler_params=pltpu.CompilerParams(
            collective_id=0, has_side_effects=True, vmem_limit_bytes=48 * 1024 * 1024
        ),
    )(
        start.reshape(big), noise.reshape(big), when, gain.reshape(1, chan), bias.reshape(1, chan),
        sw.reshape(3, 3 * chan, chan), tw, tbw,
    )
    return out.reshape(1, 1, height, width, chan)


def solution(mesh):
    placed = (
        P("frame", None, None, None),
        P("step", "frame", None, None, None),
        P("step"),
        P(),
        P(),
        P(),
        P(),
        P(),
    )
    return jax.shard_map(
        functools.partial(local, mesh.shape["step"], mesh.shape["frame"]),
        mesh=mesh,
        in_specs=placed,
        out_specs=P("step", "frame", None, None, None),
        check_vma=False,
    )
```

```python
import functools
import math

import jax
import jax.numpy as jnp
from jax import lax
from jax.experimental import pallas as pl
from jax.experimental.pallas import tpu as pltpu
from jax.sharding import PartitionSpec as P

GROUPS = 32
CHUNKS = 4
LANES = 128
MESH = pl.DeviceIdType.MESH
F32 = jnp.float32
BF16 = jnp.bfloat16


def silu(x):
    half = 0.5 * x
    return half + half * jnp.tanh(half)


def pack(v):
    n, c = v.shape
    full = c // LANES * LANES
    rest = c - full
    if not rest:
        return v.astype(BF16)
    q = n * rest // full
    tail = jnp.concatenate([v[i * q : (i + 1) * q, full:] for i in range(n // q)], axis=1)
    return jnp.concatenate([v[:, :full], tail], axis=0).astype(BF16)


def unpack(w, n, c):
    full = w.shape[1]
    rest = c - full
    w = w.astype(F32)
    if not rest:
        return w
    tail = jnp.concatenate([w[n:, i * rest : (i + 1) * rest] for i in range(full // rest)], axis=0)
    return jnp.concatenate([w[:n], tail], axis=1)


def kernel(
    steps, frames, width,
    start_in, noise_in, when, gain, bias, sw_in, tw_in, tbw_in, out,
    start, noise, sw, tw, tbw,
    tb_own, tb_all, same, x, state, act, noise_p, act_p, halo, upd, upd_p, ntot, utot, nrecv, urecv,
    load_sem, tb_send, tb_recv, h_send, h_recv, n_send, n_recv, u_send, u_recv,
):
    t = lax.axis_index("step")
    f = lax.axis_index("frame")
    cells, chan = start.shape
    size = cells // CHUNKS
    phases = len(range(0, steps.bit_length() - 1))
    has_left = f > 0
    has_right = f < frames - 1

    loads = [
        pltpu.make_async_copy(src, dst, load_sem.at[i])
        for i, (src, dst) in enumerate(
            [(noise_in, noise), (start_in, start), (tbw_in, tbw), (sw_in, sw), (tw_in, tw)]
        )
    ]
    for load in loads:
        load.start()

    barrier = pltpu.get_barrier_semaphore()
    for d in range(1, steps):
        pl.semaphore_signal(barrier, inc=1, device_id=(lax.rem(t + d, steps), f), device_id_type=MESH)

    @pl.when(has_left)
    def _():
        pl.semaphore_signal(barrier, inc=1, device_id=(t, f - 1), device_id_type=MESH)

    @pl.when(has_right)
    def _():
        pl.semaphore_signal(barrier, inc=1, device_id=(t, f + 1), device_id_type=MESH)

    pl.semaphore_wait(barrier, steps - 1 + jnp.where(has_left, 1, 0) + jnp.where(has_right, 1, 0))

    def rows(c):
        return pl.ds(c * size, size)

    packed = noise_p.shape[0] // CHUNKS

    def prows(c):
        return pl.ds(c * packed, packed)

    def bit(p):
        return lax.rem(t // (1 << p), 2)

    def swap(kind, p, c):
        own, tot, recv, ss, rs = (
            (noise_p, ntot, nrecv, n_send, n_recv) if kind == 0 else (upd_p, utot, urecv, u_send, u_recv)
        )
        src = own.at[prows(c)] if p == 0 else tot.at[p - 1, prows(c)]
        partner = t + (1 << p) * (1 - 2 * bit(p))
        return pltpu.make_async_remote_copy(
            src_ref=src, dst_ref=recv.at[p, prows(c)], send_sem=ss.at[p, c], recv_sem=rs.at[p, c],
            device_id=(partner, f), device_id_type=MESH,
        )

    def swap_do(kind, p, c, what):
        if p < phases - 1:
            what[0](swap(kind, p, c))
            return

        @pl.when(bit(p) == (0 if what[1] == "send" else 1))
        def _():
            what[0](swap(kind, p, c))

    begin = (lambda r: r.start(), "send")
    sent = (lambda r: r.wait_send(), "send")
    got = (lambda r: r.wait_recv(), "recv")

    def advance(kind, p, c):
        own, tot, recv = (noise_p, ntot, nrecv) if kind == 0 else (upd_p, utot, urecv)
        swap_do(kind, p, c, got)
        if p < phases - 1:
            have = own[prows(c), :] if p == 0 else tot[p - 1, prows(c), :]
            tot[p, prows(c), :] = (have.astype(F32) + recv[p, prows(c), :].astype(F32)).astype(BF16)
            swap_do(kind, p + 1, c, begin)

    def before(c, *recvs):
        total = jnp.zeros((packed, noise_p.shape[1]), F32)
        for recv in recvs:
            for p in range(phases):
                total = total + jnp.where(bit(p) == 1, recv[p, prows(c), :].astype(F32), 0.0)
        return unpack(total, size, chan)

    def halo_copy(sweep, side, c):
        to = f + 1 if side == 0 else f - 1
        return pltpu.make_async_remote_copy(
            src_ref=act_p.at[sweep, prows(c)], dst_ref=halo.at[sweep, side, prows(c)],
            send_sem=h_send.at[sweep, side, c], recv_sem=h_recv.at[sweep, side, c],
            device_id=(t, to), device_id_type=MESH,
        )

    def halo_do(sweep, c, what):
        send = what[1] == "send"
        for side, cond in ((0, has_right if send else has_left), (1, has_left if send else has_right)):
            @pl.when(cond)
            def _():
                what[0](halo_copy(sweep, side, c))

    loads[0].wait()
    for c in range(CHUNKS):
        noise_p[prows(c), :] = pack(noise[rows(c), :].astype(F32))
        swap_do(0, 0, c, begin)

    loads[2].wait()
    lane = lax.broadcasted_iota(jnp.int32, (8, chan), 1)
    half = tbw.shape[0] // 2
    k = jnp.where(lane < half, lane, lane - half).astype(F32)
    angle = when[0].astype(F32) * jnp.exp(-math.log(10000.0) * k / half)
    emb = jnp.where(lane < half, jnp.cos(angle), jnp.sin(angle)).astype(BF16)
    tb_own[...] = silu(jnp.dot(emb, tbw[...], preferred_element_type=F32))

    def tb_copy(d):
        return pltpu.make_async_remote_copy(
            src_ref=tb_own, dst_ref=tb_all.at[d], send_sem=tb_send.at[d], recv_sem=tb_recv.at[d],
            device_id=(lax.rem(t + d, steps), f), device_id_type=MESH,
        )

    for d in range(1, steps):
        tb_copy(d).start()

    per = chan // GROUPS
    same[...] = jnp.where(
        lax.broadcasted_iota(jnp.int32, (chan, chan), 0) // per
        == lax.broadcasted_iota(jnp.int32, (chan, chan), 1) // per, 1.0, 0.0,
    ).astype(BF16)
    pad = jnp.zeros((width, x.shape[1]), BF16)
    x[pl.ds(0, width), :] = pad
    x[pl.ds(cells + width, width), :] = pad
    for sweep in range(2):
        @pl.when(jnp.logical_not(has_left))
        def _():
            halo[sweep, 0] = jnp.zeros(noise_p.shape, BF16)

        @pl.when(jnp.logical_not(has_right))
        def _():
            halo[sweep, 1] = jnp.zeros(noise_p.shape, BF16)

    @pl.when(bit(phases - 1) == 0)
    def _():
        nrecv[phases - 1] = jnp.zeros(noise_p.shape, BF16)
        urecv[phases - 1] = jnp.zeros(noise_p.shape, BF16)

    def group_mean(total):
        row = lax.broadcasted_iota(jnp.int32, (16, chan), 0)
        hi = total.astype(BF16).astype(F32)
        mid = (total - hi).astype(BF16).astype(F32)
        low = total - hi - mid
        parts = jnp.where(row == 0, hi, jnp.where(row == 1, mid, jnp.where(row == 2, low, 0.0)))
        summed = jnp.dot(parts.astype(BF16), same[...], preferred_element_type=F32)
        return jnp.sum(summed, axis=0, keepdims=True) / (per * cells)

    def fill(ref, total):
        mean = group_mean(total)
        var = jnp.zeros((1, chan), F32)
        for c in range(CHUNKS):
            centered = ref[rows(c), :].astype(F32) - mean
            var = var + jnp.sum(centered * centered, axis=0, keepdims=True)
        scale = lax.rsqrt(group_mean(var) + 1e-05) * gain[...].reshape(1, chan)
        col = lax.rem(lax.broadcasted_iota(jnp.int32, (size, chan), 0), width)
        for c in range(CHUNKS):
            y = silu((ref[rows(c), :].astype(F32) - mean) * scale + bias[...].reshape(1, chan))
            left = jnp.where(col == 0, 0.0, pltpu.roll(y, 1, 0))
            right = jnp.where(col == width - 1, 0.0, pltpu.roll(y, size - 1, 0))
            x[pl.ds(width + c * size, size), :] = jnp.concatenate([left, y, right], axis=1).astype(BF16)

    def conv(c):
        total = None
        for i in range(3):
            term = jnp.dot(x[pl.ds(c * size + i * width, size), :], sw[i], preferred_element_type=F32)
            total = term if total is None else total + term
        return total

    def temporal(sweep, c):
        halo_do(sweep, c, got)
        total = jnp.dot(act[sweep, rows(c), :], tw[1], preferred_element_type=F32)
        for side in range(2):
            beside = unpack(halo[sweep, side, prows(c), :], size, chan).astype(BF16)
            total = total + jnp.dot(beside, tw[2 * side], preferred_element_type=F32)
        return total

    loads[1].wait()
    total = jnp.zeros((1, chan), F32)
    for c in range(CHUNKS):
        total = total + jnp.sum(start[rows(c), :].astype(F32), axis=0, keepdims=True)
    fill(start, total)
    for d in range(1, steps):
        tb_copy(d).wait()
    loads[3].wait()
    for c in range(CHUNKS):
        acc = conv(c)
        summed = jnp.zeros_like(acc)
        for d in range(1, steps):
            summed = summed + jnp.where(d <= t, silu(acc + tb_all[d, 0:1, :]), 0.0)
        act[0, rows(c), :] = summed.astype(BF16)
        act_p[0, prows(c), :] = pack(summed)
        halo_do(0, c, begin)
        if c > 0:
            advance(0, 0, c - 1)
    advance(0, 0, CHUNKS - 1)
    for p in range(1, phases - 1):
        for c in range(CHUNKS):
            advance(0, p, c)
    loads[4].wait()
    total = jnp.zeros((1, chan), F32)
    for c in range(CHUNKS):
        update = temporal(0, c)
        if phases > 1:
            advance(0, phases - 1, c)
        now = (start[rows(c), :].astype(F32) + 0.25 * (update + before(c, nrecv))).astype(BF16)
        state[rows(c), :] = now
        total = total + jnp.sum(now.astype(F32), axis=0, keepdims=True)

    fill(state, total)

    def second(c):
        update = temporal(1, c)
        upd_p[prows(c), :] = pack(update)
        upd[rows(c), :] = (update + noise[rows(c), :].astype(F32)) * 0.25 + start[rows(c), :].astype(F32)
        swap_do(1, 0, c, begin)

    for c in range(CHUNKS):
        active = silu(conv(c) + tb_own[0:1, :])
        act[1, rows(c), :] = active.astype(BF16)
        act_p[1, prows(c), :] = pack(active)
        halo_do(1, c, begin)
        if c > 1:
            second(c - 2)
    for c in range(CHUNKS - 2, CHUNKS):
        second(c)
        advance(1, 0, c - CHUNKS + 2)
    for c in range(2, CHUNKS):
        advance(1, 0, c)
    for p in range(1, phases - 1):
        for c in range(CHUNKS):
            advance(1, p, c)
    for c in range(CHUNKS):
        if phases > 1:
            advance(1, phases - 1, c)
        out[rows(c), :] = (upd[rows(c), :] + 0.25 * before(c, nrecv, urecv)).astype(BF16)

    for c in range(CHUNKS):
        for sweep in range(2):
            halo_do(sweep, c, sent)
        for kind in range(2):
            for p in range(phases):
                swap_do(kind, p, c, sent)


def local(steps, frames, start, noise, when, gain, bias, sw, tw, tbw):
    _, height, width, chan = start.shape
    cells = height * width
    phases = steps.bit_length() - 1
    big = (cells, chan)
    full = chan // LANES * LANES
    small = (cells * chan // full, full)
    hbm = pl.BlockSpec(memory_space=pltpu.HBM)
    vm = pl.BlockSpec(memory_space=pltpu.VMEM)
    dma = pltpu.SemaphoreType.DMA
    out = pl.pallas_call(
        functools.partial(kernel, steps, frames, width),
        out_shape=jax.ShapeDtypeStruct(big, BF16),
        in_specs=[hbm, hbm, pl.BlockSpec(memory_space=pltpu.SMEM), vm, vm, hbm, hbm, hbm],
        out_specs=vm,
        scratch_shapes=[
            pltpu.VMEM(big, BF16),
            pltpu.VMEM(big, BF16),
            pltpu.VMEM((3, 3 * chan, chan), BF16),
            pltpu.VMEM(tw.shape, BF16),
            pltpu.VMEM(tbw.shape, BF16),
            pltpu.VMEM((8, chan), F32),
            pltpu.VMEM((steps, 8, chan), F32),
            pltpu.VMEM((chan, chan), BF16),
            pltpu.VMEM((cells + 2 * width, 3 * chan), BF16),
            pltpu.VMEM(big, BF16),
            pltpu.VMEM((2,) + big, BF16),
            pltpu.VMEM(small, BF16),
            pltpu.VMEM((2,) + small, BF16),
            pltpu.VMEM((2, 2) + small, BF16),
            pltpu.VMEM(big, F32),
            pltpu.VMEM(small, BF16),
            pltpu.VMEM((max(phases - 1, 1),) + small, BF16),
            pltpu.VMEM((max(phases - 1, 1),) + small, BF16),
            pltpu.VMEM((phases,) + small, BF16),
            pltpu.VMEM((phases,) + small, BF16),
            dma((5,)),
            dma((steps,)), dma((steps,)),
            dma((2, 2, CHUNKS)), dma((2, 2, CHUNKS)),
            dma((phases, CHUNKS)), dma((phases, CHUNKS)),
            dma((phases, CHUNKS)), dma((phases, CHUNKS)),
        ],
        compiler_params=pltpu.CompilerParams(
            collective_id=0, has_side_effects=True, vmem_limit_bytes=48 * 1024 * 1024
        ),
    )(
        start.reshape(big), noise.reshape(big), when, gain, bias,
        sw.reshape(3, 3 * chan, chan), tw, tbw,
    )
    return out.reshape(1, 1, height, width, chan)


def solution(mesh):
    placed = (
        P("frame", None, None, None),
        P("step", "frame", None, None, None),
        P("step"),
        P(),
        P(),
        P(),
        P(),
        P(),
    )
    return jax.shard_map(
        functools.partial(local, mesh.shape["step"], mesh.shape["frame"]),
        mesh=mesh,
        in_specs=placed,
        out_specs=P("step", "frame", None, None, None),
        check_vma=False,
    )
```
